32 devices in a mesh: dp: 4 (over z), row: 4 (over y, x), col: 2 (over core).
Axes of the slice: x: 2, y: 2, z: 4, core: 2. Of those that a mesh axis runs over, the one named last changes fastest.
Arguments:
- tokens: bfloat16 [4096, 1, 960], P('dp', None, ('row', 'col')), may hold values from -6 to 6
- seg_ids: int32 [1, 4096], replicated, may hold values from 0 to 3, never falling along the last dimension, each value on 1 to 3072 neighbouring positions
- gain_one: float32 [960], P(('row', 'col')), may hold values from 0.5 to 1.5
- w_query: bfloat16 [960, 960], P('row', 'col'), may hold values from -0.1875 to 0.1875
- key_weight: bfloat16 [960, 320], P('row', 'col'), may hold values from -0.1875 to 0.1875
- value_weight: bfloat16 [960, 320], P('row', 'col'), may hold values from -0.1875 to 0.1875
- w_out: bfloat16 [960, 960], P('col', 'row'), may hold values from -0.75 to 0.75
- gain_two: float32 [960], P(('row', 'col')), may hold values from 0.5 to 1.5
- w_gate: bfloat16 [960, 2560], P('row', 'col'), may hold values from -0.1875 to 0.1875
- w_up: bfloat16 [960, 2560], P('row', 'col'), may hold values from -0.1875 to 0.1875
- w_down: bfloat16 [2560, 960], P('col', 'row'), may hold values from -0.125 to 0.125
- grad_out: bfloat16 [4096, 1, 960], P('dp', None, ('row', 'col')), may hold values from -6 to 6
Outputs:
- output: bfloat16 [4096, 1, 960], P('dp', None, ('row', 'col'))
- grad_tokens: float32 [4096, 1, 960], P('dp', None, ('row', 'col'))
- grad_gain_one: float32 [960], P(('row', 'col'))
- grad_w_query: float32 [960, 960], P('row', ('col', 'dp'))
- grad_w_key: float32 [960, 320], P('row', ('col', 'dp'))
- grad_w_value: float32 [960, 320], P('row', ('col', 'dp'))
- grad_w_out: float32 [960, 960], P(('col', 'dp'), 'row')
- grad_gain_two: float32 [960], P(('row', 'col'))
- grad_w_gate: float32 [960, 2560], P('row', ('col', 'dp'))
- grad_w_up: float32 [960, 2560], P('row', ('col', 'dp'))
- grad_w_down: float32 [2560, 960], P(('col', 'dp'), 'row')
The draws below stay inside these ranges and needn't reach their ends.
Inputs may be any that keep to these rules, and one draw needn't show every extreme that they name: Each row of seg_ids numbers the documents of one sequence from 0 upward, never falling; no document is longer than 3072 positions, and one is exactly that long.
All inputs are finite; a program needn't handle non-finite values.
Results may differ from the reference program's by a relative error of at most 0.035.
Values may be sent and summed in bfloat16 or wider, within the bound.
A program may use at most 128 MiB of HBM per device.

```python
import math
import jax
import jax.numpy as jnp
import numpy as np
from jax import lax

MODEL_WIDTH = 960
QUERY_HEADS = 15
KEY_VALUE_HEADS = 5
HEAD_SIZE = 64
FF = 2560
SEQUENCE_LENGTH = 4096
SEQUENCE_COUNT = 1
DOCS = 4


def block_levels(rng, extent, split, low, largest):
    gain, own = 1.0, jax.random.fold_in(rng, 6)
    for position, shards_of in split:
        draws = jnp.exp(jax.random.uniform(jax.random.fold_in(own, position), (shards_of,), jnp.float32, low / len(split), largest / len(split)))
        gain = gain * jnp.repeat(draws, extent[position] // shards_of).reshape([-1 if axis == position else 1 for axis in range(len(extent))])
    return gain


def length_profile(number_of, total, bound, slope):
    loads = [(1 << 20) // math.isqrt(standing ** slope) + 1 for standing in range(2, number_of + 1)]
    spare, given = total - bound - (number_of - 1), [1] * (number_of - 1)
    while spare > 0:
        free = [i for i in range(number_of - 1) if given[i] < bound]
        whole, budget = sum([loads[i] for i in free]), spare
        for i in free:
            extra = min(bound - given[i], max(1, budget * loads[i] // whole), spare)
            given[i] = given[i] + extra
            spare = spare - extra
    return np.array([bound] + given)


def uneven(own_key, number_of, total, limit, skew):
    if number_of == 2:
        one = jax.random.randint(own_key, (), max(1, total - limit), min(limit, total - 1) + 1)
        return jnp.stack([one, total - one])
    tallies = jnp.asarray(length_profile(number_of, total, limit, skew), jnp.int32)
    pairs = (number_of - 1) // 2
    giver, taker = tallies[1:1 + 2 * pairs:2], tallies[2:2 + 2 * pairs:2]
    slack = jnp.minimum(giver - 1, limit - taker)
    passed = jax.random.randint(jax.random.fold_in(own_key, 1), (pairs,), 0, 1 << 20) % (slack + 1)
    tallies = tallies.at[1:1 + 2 * pairs:2].set(giver - passed).at[2:2 + 2 * pairs:2].set(taker + passed)
    return tallies[jax.random.permutation(jax.random.fold_in(own_key, 2), number_of)]


def scatter_about(stream_key, dims, scale, most, pieces=(), kind=jnp.bfloat16):
    values = scale * jax.random.normal(stream_key, dims, jnp.float32)
    if pieces:
        values = values * block_levels(stream_key, dims, pieces, -0.22, 0.18)
    return jnp.clip(values, -most, most).astype(kind)


def setup_inputs(seed: int = 0) -> dict:
    arg_keys = jax.random.split(jax.random.key(seed), 13)
    tokens = scatter_about(arg_keys[0], (SEQUENCE_LENGTH, SEQUENCE_COUNT, MODEL_WIDTH), 1.0, 6.0, ((0, 4), (2, 8)))
    seg_ids = jax.vmap(lambda own: jnp.searchsorted(jnp.cumsum(uneven(own, DOCS, SEQUENCE_LENGTH, 3 * SEQUENCE_LENGTH // 4, 1)), jnp.arange(SEQUENCE_LENGTH), side="right"))(jax.random.split(arg_keys[1], SEQUENCE_COUNT)).reshape((SEQUENCE_COUNT, SEQUENCE_LENGTH)).astype(jnp.int32)
    gain_one = jnp.clip(1.0 + 0.1 * jax.random.normal(arg_keys[2], (MODEL_WIDTH,), jnp.float32), 0.5, 1.5)
    w_query = scatter_about(arg_keys[3], (MODEL_WIDTH, MODEL_WIDTH), MODEL_WIDTH ** -0.5, 0.1875, ((0, 4), (1, 2)))
    key_weight = scatter_about(arg_keys[4], (MODEL_WIDTH, KEY_VALUE_HEADS * HEAD_SIZE), MODEL_WIDTH ** -0.5, 0.1875, ((0, 4), (1, 2)))
    value_weight = scatter_about(arg_keys[5], (MODEL_WIDTH, KEY_VALUE_HEADS * HEAD_SIZE), MODEL_WIDTH ** -0.5, 0.1875, ((0, 4), (1, 2)))
    w_out = scatter_about(arg_keys[6], (MODEL_WIDTH, MODEL_WIDTH), (MODEL_WIDTH // 16) ** -0.5, 0.75, ((0, 2), (1, 4)))
    gain_two = jnp.clip(1.0 + 0.1 * jax.random.normal(arg_keys[7], (MODEL_WIDTH,), jnp.float32), 0.5, 1.5)
    w_gate = scatter_about(arg_keys[8], (MODEL_WIDTH, FF), MODEL_WIDTH ** -0.5, 0.1875, ((0, 4), (1, 2)))
    w_up = scatter_about(arg_keys[9], (MODEL_WIDTH, FF), MODEL_WIDTH ** -0.5, 0.1875, ((0, 4), (1, 2)))
    w_down = scatter_about(arg_keys[10], (FF, MODEL_WIDTH), FF ** -0.5, 0.125, ((0, 2), (1, 4)))
    grad_out = scatter_about(arg_keys[11], (SEQUENCE_LENGTH, SEQUENCE_COUNT, MODEL_WIDTH), 1.0, 6.0, ((0, 4), (2, 8)))
    return dict(tokens=tokens, seg_ids=seg_ids, gain_one=gain_one, w_query=w_query, key_weight=key_weight, value_weight=value_weight, w_out=w_out, gain_two=gain_two, w_gate=w_gate, w_up=w_up, w_down=w_down, grad_out=grad_out)


EPSILON = 1e-05
ROPE_BASE = 100000.0
MASKED = -1e+30
HIGHEST = lax.Precision.HIGHEST

@jax.custom_vjp
def low(v):
    return lax.optimization_barrier(v.astype(jnp.bfloat16)).astype(jnp.float32)

@jax.custom_vjp
def low_back(v):
    return v

def low_keep(v):
    return (low(v), None)

def low_pass(kept, grad):
    return (grad,)

def back_keep(v):
    return (v, None)

def back_low(kept, grad):
    return (low(grad),)
low.defvjp(low_keep, low_pass)
low_back.defvjp(back_keep, back_low)

def rms_scale(stream, gain_vec):
    return stream * lax.rsqrt(lax.optimization_barrier(jnp.mean(stream * stream, axis=-1, keepdims=True)) + EPSILON) * gain_vec

def positions(segment_labels):
    labels = jnp.arange(DOCS, dtype=jnp.int32)
    member = (segment_labels[:, :, None] == labels[None, None, :]).astype(jnp.int32)
    counts = lax.optimization_barrier(jnp.sum(member, axis=1))
    starts = jnp.cumsum(counts, axis=1) - counts
    first_pos = lax.optimization_barrier(jnp.sum(member * starts[:, None, :], axis=2))
    position_index = jnp.arange(segment_labels.shape[1], dtype=jnp.int32)
    return position_index[None, :] - first_pos

def apply_rotary(inputs, token_positions, direction):
    half_dim = inputs.shape[-1] // 2
    frequency = jnp.power(ROPE_BASE, -jnp.arange(half_dim, dtype=jnp.float32) * (2.0 / inputs.shape[-1]))
    angles = jnp.transpose(token_positions).astype(jnp.float32)[:, :, None, None] * frequency
    cosine = jnp.cos(angles)
    sine_part = jnp.sin(angles) * direction
    first_half = inputs[..., :half_dim]
    second_half = inputs[..., half_dim:]
    return jnp.concatenate([first_half * cosine - second_half * sine_part, second_half * cosine + first_half * sine_part], axis=-1)

def attention_layer(query_head_rows, key_head_rows, value_head_rows, segment_labels):
    heads_per_group = QUERY_HEADS // KEY_VALUE_HEADS
    query_block_length = min(256, SEQUENCE_LENGTH)
    count_of_blocks = SEQUENCE_LENGTH // query_block_length
    score_scale = 1.0 / math.sqrt(HEAD_SIZE)
    blocked_rows = query_head_rows.reshape(count_of_blocks, query_block_length, SEQUENCE_COUNT, KEY_VALUE_HEADS, heads_per_group, HEAD_SIZE)
    position_index = jnp.arange(SEQUENCE_LENGTH, dtype=jnp.int32)

    def attend_block(inputs):
        query_block, offset = inputs
        scores = jnp.einsum('qsgjd,ksgd->sgjqk', query_block, key_head_rows, precision=HIGHEST) * score_scale
        query_index = offset + jnp.arange(query_block_length, dtype=jnp.int32)
        query_segs = lax.dynamic_slice_in_dim(segment_labels, offset, query_block_length, 1)
        allowed = (query_segs[:, :, None] == segment_labels[:, None, :]) & (position_index[None, None, :] <= query_index[None, :, None])
        scores = low_back(jnp.where(allowed[:, None, None], scores, MASKED))
        highest = lax.optimization_barrier(jnp.max(scores, axis=-1, keepdims=True))
        weights = jnp.exp(scores - highest)
        probability = weights / lax.optimization_barrier(jnp.sum(weights, axis=-1, keepdims=True))
        return jnp.einsum('sgjqk,ksgd->qsgjd', low(probability), value_head_rows, precision=HIGHEST)
    offsets = jnp.arange(count_of_blocks, dtype=jnp.int32) * query_block_length
    result = lax.map(jax.checkpoint(attend_block), (blocked_rows, offsets))
    return result.reshape(SEQUENCE_LENGTH, SEQUENCE_COUNT, QUERY_HEADS * HEAD_SIZE)

def project(inputs, matrix):
    return jnp.einsum('lsd,de->lse', inputs, matrix, precision=HIGHEST)

def block_forward(tokens, gain_one, w_query, key_weight, value_weight, w_out, gain_two, w_gate, w_up, w_down, token_positions, segment_labels):
    normed = low(rms_scale(tokens, gain_one))
    query_raw = low_back(low(project(normed, w_query)))
    key_unrotated = low_back(low(project(normed, key_weight)))
    value_projected = low_back(low(project(normed, value_weight)))
    query_head_rows = low(apply_rotary(query_raw.reshape(SEQUENCE_LENGTH, SEQUENCE_COUNT, QUERY_HEADS, HEAD_SIZE), token_positions, 1.0))
    key_head_rows = low(apply_rotary(key_unrotated.reshape(SEQUENCE_LENGTH, SEQUENCE_COUNT, KEY_VALUE_HEADS, HEAD_SIZE), token_positions, 1.0))
    value_head_rows = value_projected.reshape(SEQUENCE_LENGTH, SEQUENCE_COUNT, KEY_VALUE_HEADS, HEAD_SIZE)
    attended_output = attention_layer(query_head_rows.reshape(SEQUENCE_LENGTH, SEQUENCE_COUNT, KEY_VALUE_HEADS, QUERY_HEADS // KEY_VALUE_HEADS, HEAD_SIZE), key_head_rows, value_head_rows, segment_labels)
    attended_output = low_back(low(attended_output))
    middle = tokens + low_back(project(attended_output, w_out))
    second = low(rms_scale(middle, gain_two))
    gate_values = low_back(project(second, w_gate))
    up_values = low_back(project(second, w_up))
    hidden = low(jax.nn.silu(gate_values) * up_values)
    return middle + low_back(project(hidden, w_down))

def reference(tokens, seg_ids, gain_one, w_query, key_weight, value_weight, w_out, gain_two, w_gate, w_up, w_down, grad_out):
    token_positions = positions(seg_ids)
    floats = [array_in.astype(jnp.float32) for array_in in (tokens, gain_one, w_query, key_weight, value_weight, w_out, gain_two, w_gate, w_up, w_down)]

    def forward(*inputs):
        return block_forward(*inputs, token_positions, seg_ids)
    output, pullback = jax.vjp(forward, *floats)
    gradients = pullback(grad_out.astype(jnp.float32))
    return (output.astype(jnp.bfloat16), gradients[0], gradients[1], gradients[2], gradients[3], gradients[4], gradients[5], gradients[6], gradients[7], gradients[8], gradients[9])
```

```python
import functools
import math

import jax
import jax.numpy as jnp
from jax import lax
from jax.experimental import pallas as pl
from jax.experimental.pallas import tpu as pltpu
from jax.sharding import PartitionSpec as P

MODEL_WIDTH = 960
QUERY_HEADS = 15
KEY_VALUE_HEADS = 5
HEAD_SIZE = 64
GROUP = QUERY_HEADS // KEY_VALUE_HEADS
DOCS = 4
EPSILON = 1e-05
ROPE_BASE = 100000.0
MASKED = -1e30
MESH = pl.DeviceIdType.MESH
F32 = jnp.float32
BF16 = jnp.bfloat16


def positions_start(segment_labels):
    labels = jnp.arange(DOCS, dtype=jnp.int32)
    member = (segment_labels[:, :, None] == labels[None, None, :]).astype(jnp.int32)
    counts = jnp.sum(member, axis=1)
    starts = jnp.cumsum(counts, axis=1) - counts
    return jnp.sum(member * starts[:, None, :], axis=2)[0]


def rotary(inputs, cosine, sine):
    first_half = inputs[..., :32]
    second_half = inputs[..., 32:]
    return jnp.concatenate(
        [
            first_half * cosine - second_half * sine,
            second_half * cosine + first_half * sine,
        ],
        axis=-1,
    )


def exchange_kernel(axes, sizes, modes, offsets, counts, *refs):
    k = len(modes)
    ins, outs = refs[:k], refs[k : 2 * k]
    send, recv, local = refs[2 * k :]
    here = [lax.axis_index(a) for a in axes]

    def source(i, place):
        how, span = modes[i]
        if how == "whole":
            return ins[i]
        if how == "lead":
            return ins[i].at[place[0]]
        return ins[i].at[tuple(place[:span])]

    barrier = pltpu.get_barrier_semaphore()
    places = []
    for off in offsets:
        place = [lax.rem(h + o, s) for h, o, s in zip(here, off, sizes)]
        places.append(place)
        pl.semaphore_signal(
            barrier, inc=1, device_id=dict(zip(axes, place)), device_id_type=MESH
        )
    pl.semaphore_wait(barrier, len(offsets))
    copies = []
    slot = 0
    for off, place in zip(offsets, places):
        for i, (how, span) in enumerate(modes):
            if any(off[span:]):
                continue
            copy = pltpu.make_async_remote_copy(
                src_ref=source(i, place),
                dst_ref=outs[i].at[tuple(here[:span])],
                send_sem=send.at[slot],
                recv_sem=recv.at[slot],
                device_id=dict(zip(axes, place)),
                device_id_type=MESH,
            )
            copy.start()
            copies.append(copy)
            slot += 1
    for i, (how, span) in enumerate(modes):
        copy = pltpu.make_async_copy(
            source(i, here), outs[i].at[tuple(here[:span])], local.at[i]
        )
        copy.start()
        copies.append(copy)
    for copy in copies:
        copy.wait()


def exchange(number, axes, parts):
    sizes = [lax.axis_size(a) for a in axes]
    offsets = [()]
    for s in sizes:
        offsets = [o + (j,) for o in offsets for j in range(s)]
    offsets = [o for o in offsets if any(o)]
    modes = [(how, span) for how, span, _ in parts]
    arrays = [a for _, _, a in parts]
    shapes = []
    for how, span, a in parts:
        lead = {"whole": 0, "lead": 1, "block": span}[how]
        shapes.append(jax.ShapeDtypeStruct(tuple(sizes[:span]) + a.shape[lead:], a.dtype))
    slots = sum(1 for o in offsets for _, span in modes if not any(o[span:]))
    any_spec = pl.BlockSpec(memory_space=pl.ANY)
    return pl.pallas_call(
        functools.partial(exchange_kernel, axes, sizes, modes, offsets, None),
        out_shape=shapes,
        in_specs=[any_spec] * len(arrays),
        out_specs=[any_spec] * len(arrays),
        scratch_shapes=[
            pltpu.SemaphoreType.DMA((slots,)),
            pltpu.SemaphoreType.DMA((slots,)),
            pltpu.SemaphoreType.DMA((len(arrays),)),
        ],
        compiler_params=pltpu.CompilerParams(collective_id=number, has_side_effects=True),
        name="exchange_%d" % number,
    )(*arrays)


def dot(a, b, ca, cb):
    return lax.dot_general(a, b, (((ca,), (cb,)), ((), ())), preferred_element_type=F32)


def block_mask(step, block, lo_ref, hi_ref, rows):
    index = step * block + lax.broadcasted_iota(jnp.int32, (rows, block), 1)
    return (index >= lo_ref[...]) & (index <= hi_ref[...])


def forward_kernel(block, span_ref, q_ref, kv_ref, lo_ref, hi_ref, o_ref, lse_ref):
    rows = q_ref.shape[1]
    q = q_ref[0]

    def step(j, carry):
        high, total, acc = carry
        kv = kv_ref[pl.ds(pl.multiple_of(j * block, block), block), :]
        ok = block_mask(j, block, lo_ref, hi_ref, rows)
        scores = jnp.where(ok, dot(q, kv, 1, 1), MASKED)
        raised = jnp.maximum(high, jnp.max(scores, axis=1, keepdims=True))
        weight = jnp.exp(scores - raised)
        scale = jnp.exp(high - raised)
        total = total * scale + jnp.sum(weight, axis=1, keepdims=True)
        acc = acc * scale + dot(weight.astype(BF16), kv, 1, 0)
        return raised, total, acc

    init = (
        jnp.full((rows, 1), MASKED, F32),
        jnp.zeros((rows, 1), F32),
        jnp.zeros((rows, 128), F32),
    )
    high, total, acc = lax.fori_loop(span_ref[0], span_ref[1], step, init)
    o_ref[0] = acc / total
    lse_ref[0] = high + jnp.log(total)


def backward_kernel(
    block, span_ref, q_ref, do_ref, kv_ref, lo_ref, hi_ref, lse_ref, delta_ref, dq_ref, dkv_ref
):
    rows = q_ref.shape[1]
    q = q_ref[0]
    do = do_ref[0]
    lse = lse_ref[0]
    delta = delta_ref[0]
    dkv_ref[...] = jnp.zeros_like(dkv_ref)

    def step(j, acc):
        at = pl.ds(pl.multiple_of(j * block, block), block)
        kv = kv_ref[at, :]
        ok = block_mask(j, block, lo_ref, hi_ref, rows)
        scores = jnp.where(ok, dot(q, kv, 1, 1), MASKED)
        prob = jnp.exp(scores - lse)
        gs = (prob * (dot(do, kv, 1, 1) - delta)).astype(BF16)
        dkv_ref[at, :] = (dot(gs, q, 0, 0) + dot(prob.astype(BF16), do, 0, 0)).astype(BF16)
        return acc + dot(gs, kv, 1, 0)

    dq_ref[0] = lax.fori_loop(
        span_ref[0], span_ref[1], step, jnp.zeros((rows, 128), F32)
    )


def attention_specs(rows, length):
    head = pl.BlockSpec((1, rows, 128), lambda g, s: (g, 0, 0))
    kv = pl.BlockSpec((length, 128), lambda g, s: (0, g))
    bound = pl.BlockSpec((rows, 1), lambda g, s: (0, 0))
    stat = pl.BlockSpec((1, rows, 1), lambda g, s: (g, 0, 0))
    return head, kv, bound, stat


def attention_forward(span, q, kv, lo, hi, block):
    heads, rows, _ = q.shape
    head, kvs, bound, stat = attention_specs(rows, kv.shape[0])
    return pl.pallas_call(
        functools.partial(forward_kernel, block),
        grid_spec=pltpu.PrefetchScalarGridSpec(
            num_scalar_prefetch=1,
            grid=(heads,),
            in_specs=[head, kvs, bound, bound],
            out_specs=[head, stat],
        ),
        out_shape=[
            jax.ShapeDtypeStruct((heads, rows, 128), F32),
            jax.ShapeDtypeStruct((heads, rows, 1), F32),
        ],
        compiler_params=pltpu.CompilerParams(vmem_limit_bytes=40 * 2**20),
        name="attend",
    )(span, q, kv, lo, hi)


def attention_backward(span, q, do, kv, lo, hi, lse, delta, block):
    heads, rows, _ = q.shape
    head, kvs, bound, stat = attention_specs(rows, kv.shape[0])
    return pl.pallas_call(
        functools.partial(backward_kernel, block),
        grid_spec=pltpu.PrefetchScalarGridSpec(
            num_scalar_prefetch=1,
            grid=(heads,),
            in_specs=[head, head, kvs, bound, bound, stat, stat],
            out_specs=[head, kvs],
        ),
        out_shape=[
            jax.ShapeDtypeStruct((heads, rows, 128), F32),
            jax.ShapeDtypeStruct(kv.shape, BF16),
        ],
        compiler_params=pltpu.CompilerParams(vmem_limit_bytes=40 * 2**20),
        name="attend_back",
    )(span, q, do, kv, lo, hi, lse, delta)


def norm(x, gain):
    inverse = lax.rsqrt(jnp.mean(x * x, axis=1, keepdims=True) + EPSILON)
    return inverse, (x * inverse * gain).astype(BF16)


def norm_back(x, gain, inverse, grad):
    weighted = grad * gain
    inner = jnp.sum(weighted * x, axis=1, keepdims=True)
    back = inverse * weighted - x * (inverse * inverse * inverse * inner / MODEL_WIDTH)
    return back, jnp.sum(grad * x * inverse, axis=0)


def pad8(v):
    return jnp.broadcast_to(v[None, :], (8,) + v.shape)


def total32(a, axis=0):
    return jnp.sum(a.astype(F32), axis=axis)


def shards(
    tokens,
    seg_ids,
    gain_one,
    w_query,
    key_weight,
    value_weight,
    w_out,
    gain_two,
    w_gate,
    w_up,
    w_down,
    grad_out,
):
    length, sequences, part = tokens.shape
    dps, rows, cols = (lax.axis_size(a) for a in ("dp", "row", "col"))
    chip_len = length // rows
    own = chip_len // cols
    col = lax.axis_index("col")
    qc, kc, half = w_query.shape[1], key_weight.shape[1], w_gate.shape[1]
    row_block = w_query.shape[0]
    width = row_block * rows

    pair_block = jnp.concatenate([w_gate, w_up], axis=1)
    w_pair = lax.all_gather(pair_block, "row", axis=0, tiled=True)
    w_down_half = lax.all_gather(w_down, "row", axis=1, tiled=True)

    joined_block = jnp.concatenate([w_query, key_weight, value_weight], axis=1)
    gains_in = jnp.concatenate([pad8(gain_one), pad8(gain_two)], axis=0)
    x_parts, g_parts, gain_parts, joined_rows, out_cols = exchange(
        0,
        ("row", "col"),
        [
            ("lead", 2, tokens.reshape(rows, chip_len, part)),
            ("lead", 2, grad_out.reshape(rows, chip_len, part)),
            ("whole", 2, gains_in),
            ("whole", 1, joined_block),
            ("whole", 1, w_out),
        ],
    )
    joined_all, out_all = exchange(
        1, ("col",), [("whole", 1, joined_rows), ("whole", 1, out_cols)]
    )
    w_joined = jnp.transpose(joined_all, (1, 2, 0, 3)).reshape(width, cols, -1)
    w_q = w_joined[:, :, :qc].reshape(width, cols * qc)
    w_k = w_joined[:, :, qc : qc + kc].reshape(width, cols * kc)
    w_v = w_joined[:, :, qc + kc :].reshape(width, cols * kc)
    w_qkv = jnp.concatenate([w_q, w_k, w_v], axis=1)
    w_o = jnp.transpose(out_all, (0, 2, 1, 3)).reshape(cols * w_out.shape[0], width)

    gain_parts = gain_parts.reshape(rows * cols, 2, 8, part)[:, :, 0]
    gain1 = gain_parts[:, 0].reshape(1, width)
    gain2 = gain_parts[:, 1].reshape(1, width)
    x_chip = jnp.transpose(x_parts, (2, 0, 1, 3)).reshape(chip_len, width).astype(F32)
    g_chip = jnp.transpose(g_parts, (2, 0, 1, 3)).reshape(chip_len, width)
    x_own = lax.dynamic_slice_in_dim(x_chip, col * own, own, 0)
    g_own = lax.dynamic_slice_in_dim(g_chip, col * own, own, 0).astype(F32)

    normed_one_chip = norm(x_chip, gain1)[1]
    inverse_one, normed_one = norm(x_own, gain1)
    qkv = dot(normed_one, w_qkv, 1, 0).astype(BF16).astype(F32)

    first_pos = lax.axis_index(("dp", "row", "col")) * own
    starts = positions_start(seg_ids)
    my_start = lax.dynamic_slice_in_dim(starts, first_pos, own, 0)
    my_index = first_pos + jnp.arange(own, dtype=jnp.int32)
    places = my_index - my_start
    frequency = jnp.power(ROPE_BASE, -jnp.arange(32, dtype=F32) * (2.0 / HEAD_SIZE))
    angles = places.astype(F32)[:, None, None] * frequency
    cosine, sine = jnp.cos(angles), jnp.sin(angles)
    nq, nk = QUERY_HEADS * HEAD_SIZE, KEY_VALUE_HEADS * HEAD_SIZE
    q = rotary(qkv[:, :nq].reshape(own, QUERY_HEADS, HEAD_SIZE), cosine, sine).astype(BF16)
    k = rotary(qkv[:, nq : nq + nk].reshape(own, KEY_VALUE_HEADS, HEAD_SIZE), cosine, sine)
    v = qkv[:, nq + nk :].reshape(own, KEY_VALUE_HEADS, HEAD_SIZE)
    kv = jnp.concatenate([k, v], axis=-1).astype(BF16).reshape(own, KEY_VALUE_HEADS * 128)

    (kv_dp,) = exchange(2, ("dp",), [("whole", 1, kv)])
    (kv_row,) = exchange(3, ("row",), [("whole", 1, kv_dp)])
    (kv_col,) = exchange(4, ("col",), [("whole", 1, kv_row)])
    full = own * dps * rows * cols
    kv_all = jnp.transpose(kv_col, (2, 1, 0, 3, 4)).reshape(full, KEY_VALUE_HEADS * 128)

    def to_heads(a):
        a = a.reshape(own, KEY_VALUE_HEADS, GROUP, HEAD_SIZE)
        return jnp.transpose(a, (1, 2, 0, 3)).reshape(KEY_VALUE_HEADS, GROUP * own, HEAD_SIZE)

    def from_heads(a):
        a = a.reshape(KEY_VALUE_HEADS, GROUP, own, HEAD_SIZE)
        return jnp.transpose(a, (2, 0, 1, 3)).reshape(own, nq)

    block = min(512, full)
    scale = 1.0 / math.sqrt(HEAD_SIZE)
    q_heads = to_heads(q)
    empty = jnp.zeros_like(q_heads)
    q_pad = jnp.concatenate([q_heads * jnp.asarray(scale, BF16), empty], axis=-1)
    lo = jnp.tile(my_start, GROUP)[:, None]
    hi = jnp.tile(my_index, GROUP)[:, None]
    span = jnp.stack([my_start[0] // block, my_index[-1] // block + 1]).astype(jnp.int32)
    o_pad, lse = attention_forward(span, q_pad, kv_all, lo, hi, block)
    attended = o_pad[:, :, HEAD_SIZE:]
    attn = from_heads(attended.astype(BF16))

    middle = x_own + dot(attn, w_o, 1, 0)
    inverse_two, normed_two = norm(middle, gain2)
    (normed_two_chip,) = exchange(5, ("col",), [("whole", 1, normed_two)])
    normed_two_chip = normed_two_chip.reshape(chip_len, width)
    gate_up = dot(normed_two_chip, w_pair, 1, 0)
    gate, up = gate_up[:, :half], gate_up[:, half:]
    sig = jax.nn.sigmoid(gate)
    hidden = (gate * sig * up).astype(BF16)
    out_part = dot(hidden, w_down_half, 1, 0).astype(BF16)
    grad_hidden = dot(g_chip, w_down_half, 1, 1)
    grad_gate = grad_hidden * up * sig * (1.0 + gate * (1.0 - sig))
    grad_up = grad_hidden * gate * sig
    grad_pair = jnp.concatenate([grad_gate, grad_up], axis=1).astype(BF16)
    back_part = dot(grad_pair, w_pair, 1, 1).astype(BF16)
    out_parts, back_parts = exchange(
        6,
        ("col",),
        [
            ("block", 1, out_part.reshape(cols, own, width)),
            ("block", 1, back_part.reshape(cols, own, width)),
        ],
    )
    output_own = (middle + total32(out_parts)).astype(BF16)

    gw_pair = dot(normed_two_chip, grad_pair, 0, 0).astype(BF16)
    gw_down = dot(hidden, g_chip, 0, 0).astype(BF16)
    gw_pair = lax.psum_scatter(gw_pair, "row", scatter_dimension=0, tiled=True)
    gw_down = lax.psum_scatter(gw_down, "row", scatter_dimension=1, tiled=True)

    back_two, gg_two = norm_back(middle, gain2, inverse_two, total32(back_parts))
    grad_middle = g_own + back_two
    grad_branch = grad_middle.astype(BF16)
    grad_attn = dot(grad_branch, w_o, 1, 1).astype(BF16)
    do_heads = to_heads(grad_attn)
    delta = jnp.sum(do_heads.astype(F32) * attended, axis=-1, keepdims=True)
    do_pad = jnp.concatenate([empty, do_heads], axis=-1)
    dq_pad, dkv = attention_backward(span, q_pad, do_pad, kv_all, lo, hi, lse, delta, block)

    dkv = dkv.reshape(dps, rows, cols, own, KEY_VALUE_HEADS * 128)
    dkv = jnp.transpose(dkv, (2, 1, 0, 3, 4))
    attn_halves = jnp.transpose(attn.reshape(own, cols, -1), (1, 0, 2))
    dkv_c, attn_c, branch_c = exchange(
        7, ("col",), [("block", 1, dkv), ("block", 1, attn_halves), ("whole", 1, grad_branch)]
    )
    (dkv_r,) = exchange(8, ("row",), [("block", 1, total32(dkv_c).astype(BF16))])
    (dkv_d,) = exchange(9, ("dp",), [("block", 1, total32(dkv_r).astype(BF16))])
    dkv_own = total32(dkv_d).reshape(own, KEY_VALUE_HEADS, 128)
    dq = from_heads(dq_pad[:, :, :HEAD_SIZE]).reshape(own, QUERY_HEADS, HEAD_SIZE) * scale
    dq = rotary(dq, cosine, -sine).astype(BF16).reshape(own, nq)
    dk = rotary(dkv_own[:, :, :HEAD_SIZE], cosine, -sine).astype(BF16).reshape(own, nk)
    dv = dkv_own[:, :, HEAD_SIZE:].astype(BF16).reshape(own, nk)
    grad_qkv = jnp.concatenate([dq, dk, dv], axis=1)
    grad_halves = jnp.concatenate(
        [a.reshape(own, cols, -1) for a in (dq, dk, dv)], axis=2
    )
    (grad_half,) = exchange(
        10, ("col",), [("block", 1, jnp.transpose(grad_halves, (1, 0, 2)))]
    )
    gw_joined = dot(normed_one_chip, grad_half.reshape(chip_len, -1), 0, 0).astype(BF16)
    gw_out = dot(
        branch_c.reshape(chip_len, width), attn_c.reshape(chip_len, -1), 0, 0
    ).astype(BF16)
    back_one, gg_one = norm_back(x_own, gain1, inverse_one, dot(grad_qkv, w_qkv, 1, 1))
    grad_x = grad_middle + back_one

    def by_owner(a):
        return jnp.transpose(a.reshape(own, rows, cols, part), (1, 2, 0, 3))

    gains = jnp.stack([gg_one, gg_two]).reshape(2, rows, cols, part)
    gains = jnp.broadcast_to(jnp.transpose(gains, (1, 2, 0, 3))[:, :, :, None], (rows, cols, 2, 8, part))
    gw_joined, gw_out, output, grad_tokens, gains = exchange(
        11,
        ("row", "col"),
        [
            ("block", 1, gw_joined.reshape(rows, row_block, -1)),
            ("block", 1, gw_out.reshape(rows, row_block, -1)),
            ("block", 2, by_owner(output_own)),
            ("block", 2, by_owner(grad_x)),
            ("block", 2, gains),
        ],
    )
    gw_joined = total32(gw_joined).astype(BF16)
    gw_out = total32(gw_out).astype(BF16)
    gains = jnp.sum(gains, axis=(0, 1))

    def over_dp(a):
        return jnp.transpose(a.reshape(a.shape[0], dps, -1), (1, 0, 2))

    joined = jnp.concatenate(
        [
            over_dp(gw_joined[:, :qc]),
            over_dp(gw_joined[:, qc : qc + kc]),
            over_dp(gw_joined[:, qc + kc :]),
            over_dp(gw_out),
        ],
        axis=2,
    )
    ffn = jnp.concatenate([over_dp(gw_pair[:, :half]), over_dp(gw_pair[:, half:])], axis=2)
    joined, ffn, down, gains = exchange(
        12,
        ("dp",),
        [
            ("block", 1, joined),
            ("block", 1, ffn),
            ("block", 1, gw_down.reshape(dps, half // dps, row_block)),
            ("whole", 1, gains),
        ],
    )
    joined, ffn, down = total32(joined), total32(ffn), total32(down)
    gains = jnp.sum(gains, axis=0)[:, 0]
    qd, kd = qc // dps, kc // dps
    return (
        output.reshape(length, sequences, part),
        grad_tokens.reshape(length, sequences, part),
        gains[0],
        joined[:, :qd],
        joined[:, qd : qd + kd],
        joined[:, qd + kd : qd + 2 * kd],
        joined[:, qd + 2 * kd :].T,
        gains[1],
        ffn[:, : half // dps],
        ffn[:, half // dps :],
        down,
    )


def solution(mesh):
    in_specs = (
        P("dp", None, ("row", "col")),
        P(),
        P(("row", "col")),
        P("row", "col"),
        P("row", "col"),
        P("row", "col"),
        P("col", "row"),
        P(("row", "col")),
        P("row", "col"),
        P("row", "col"),
        P("col", "row"),
        P("dp", None, ("row", "col")),
    )
    out_specs = (
        P("dp", None, ("row", "col")),
        P("dp", None, ("row", "col")),
        P(("row", "col")),
        P("row", ("col", "dp")),
        P("row", ("col", "dp")),
        P("row", ("col", "dp")),
        P(("col", "dp"), "row"),
        P(("row", "col")),
        P("row", ("col", "dp")),
        P("row", ("col", "dp")),
        P(("col", "dp"), "row"),
    )
    return jax.shard_map(shards, mesh=mesh, in_specs=in_specs, out_specs=out_specs, check_vma=False)
```
